32 devices in a mesh: seq: 8 (over z, x), hg: 4 (over y, core).
Axes of the slice: x: 2, y: 2, z: 4, core: 2. Of those that a mesh axis runs over, the one named last changes fastest.
Arguments:
- conv_input: bfloat16 [16384, 4096], P('seq', 'hg'), may hold values from -6 to 6
- grad_output: bfloat16 [16384, 4096], P('seq', 'hg'), may hold values from -0.015625 to 0.015625
- inject: bfloat16 [16384, 128], P('seq'), may hold values from -6 to 6
- readout: bfloat16 [16384, 128], P('seq'), may hold values from -6 to 6
- conv_weight: bfloat16 [4, 4096], P(None, 'hg'), may hold values from -3 to 3
- decay_codes: int32 [64, 64], P('hg', 'seq'), may hold values from 0 to 1000, as said below
Outputs:
- grad_input: float32 [16384, 4096], P('seq', 'hg')
- grad_inject: float32 [16384, 128], P('seq')
- grad_readout: float32 [16384, 128], P('seq')
The draws below stay inside these ranges and needn't reach their ends.
Inputs may be any that keep to these rules, and one draw needn't show every extreme that they name: The decay of every step of span c in head h is 1 - 1e-6 decay_codes[h, c].
All inputs are finite; a program needn't handle non-finite values.
Results may differ from the reference program's by a relative error of at most 0.0029.
Values may be sent and summed in bfloat16 or wider, within the bound.
A program may use at most 128 MiB of HBM per device.

```python
import jax
import jax.numpy as jnp
from jax import lax

HEADS = 64
HEAD_DIM = 64
STATE = 128
TOKENS = 16384
NCH = 64


def draw_decay_codes(key, part):
    key_head, key_span, key_spot, key_zero = jax.random.split(key, 4)
    powers = jax.random.randint(key_head, (HEADS, 1), 0, 11)
    limits = jnp.left_shift(jnp.ones((HEADS, 1), jnp.int32), powers)
    drawn = jax.random.randint(key_span, (HEADS, NCH), 0, 1 << 30)
    code_table = jnp.minimum(drawn % (limits + 1), 1000)
    position = jax.random.randint(key_spot, (), 0, HEADS * NCH)
    zero_spot = jax.random.randint(key_zero, (), 0, HEADS * NCH)
    flattened = code_table.reshape(-1).at[zero_spot].set(0).at[position].set(1000)
    return flattened.reshape(HEADS, NCH).astype(jnp.int32)


def block_levels(stream_key, shape, cuts, least, top_value):
    loudness, own = 1.0, jax.random.fold_in(stream_key, 6)
    for dim, shards_of in cuts:
        draws = jnp.exp(jax.random.uniform(jax.random.fold_in(own, dim), (shards_of,), jnp.float32, least / len(cuts), top_value / len(cuts)))
        loudness = loudness * jnp.repeat(draws, shape[dim] // shards_of).reshape([-1 if axis == dim else 1 for axis in range(len(shape))])
    return loudness


def normal_values(stream_key, shape, scale, bound, cuts=(), held_as=jnp.bfloat16):
    entries = jax.random.normal(stream_key, shape, jnp.float32) * scale
    if len(cuts) > 0:
        entries = block_levels(stream_key, shape, cuts, -0.22, 0.18) * entries
    return jnp.clip(entries, min=-bound, max=bound).astype(held_as)


def setup_inputs(seed: int = 0) -> dict:
    seeds = jax.random.split(jax.random.key(seed), 7)
    return {
        "conv_input": normal_values(seeds[0], (TOKENS, HEADS * HEAD_DIM), 1.0, 6.0, ((0, 8), (1, 4))),
        "grad_output": normal_values(seeds[1], (TOKENS, HEADS * HEAD_DIM), 0.001, 0.015625, ((0, 8), (1, 4))),
        "inject": normal_values(seeds[2], (TOKENS, STATE), 1.0, 6.0, ((0, 8),)),
        "readout": normal_values(seeds[3], (TOKENS, STATE), 1.0, 6.0, ((0, 8),)),
        "conv_weight": normal_values(seeds[4], (4, HEADS * HEAD_DIM), 4 ** -0.5, 3.0, ((1, 4),)),
        "decay_codes": draw_decay_codes(jax.random.fold_in(seeds[6], 71), 0),
    }


precise = lax.Precision.HIGHEST


def causal_conv(padded, weights, length):
    summed = weights[0] * padded[0:length].astype(jnp.float32)
    for offset in range(1, 4):
        summed = summed + weights[offset] * padded[offset:offset + length].astype(jnp.float32)
    return summed


def silu_slope(preact):
    squashed = jax.nn.sigmoid(preact)
    return squashed * (1.0 + preact * (1.0 - squashed))


def span_terms(block_act, block_grad, block_inject, block_readout, block_rates, grad_after):
    span_len = block_act.shape[0]
    places = jnp.arange(span_len).astype(jnp.float32)
    spread = places[:, None] - places[None, :]
    decay_mask = jnp.where(spread[None] >= 0.0, jnp.exp(jnp.maximum(spread, 0.0)[None] * block_rates[:, None, None]), 0.0)
    products = jnp.dot(block_readout, block_inject.T, preferred_element_type=jnp.float32)
    mixing = (products[None] * decay_mask).astype(jnp.bfloat16)
    grad_act = jnp.einsum("hji,jhp->ihp", mixing.astype(jnp.float32), block_grad.astype(jnp.float32))
    pair_weights = (jnp.einsum("ihp,jhp->hij", block_grad.astype(jnp.float32), block_act.astype(jnp.float32)) * decay_mask).astype(jnp.bfloat16)
    grad_readout = jnp.einsum("hij,jn->in", pair_weights.astype(jnp.float32), block_inject.astype(jnp.float32))
    grad_inject = jnp.einsum("hij,in->jn", pair_weights.astype(jnp.float32), block_readout.astype(jnp.float32))
    tail_decay = jnp.exp((span_len - 1.0 - places)[:, None] * block_rates[None, :])
    grad_act = grad_act + jnp.einsum("qn,hpn->qhp", block_inject.astype(jnp.float32), grad_after, precision=precise) * tail_decay[:, :, None]
    grad_inject = grad_inject + jnp.einsum("qhp,hpn->qn", block_act.astype(jnp.float32) * tail_decay[:, :, None], grad_after, precision=precise)
    return grad_act, grad_inject, grad_readout


def reference(conv_input, grad_output, inject, readout, conv_weight, decay_codes):
    tokens, channels = conv_input.shape
    head_count, spans = decay_codes.shape
    span_len = tokens // spans
    head_dim = channels // head_count
    states = inject.shape[1]
    weights = conv_weight.astype(jnp.float32)
    padded = jnp.concatenate([jnp.zeros((3, channels), jnp.bfloat16), conv_input], axis=0)
    preact = causal_conv(padded, weights, tokens)
    activated = jax.nn.silu(preact).astype(jnp.bfloat16)
    log_rates = jnp.log1p(-decay_codes.astype(jnp.float32) * 1e-6)
    act_blocks = activated.reshape(spans, span_len, head_count, head_dim)
    grad_blocks = grad_output.reshape(spans, span_len, head_count, head_dim)
    inject_blocks = inject.reshape(spans, span_len, states)
    readout_blocks = readout.reshape(spans, span_len, states)
    rate_blocks = log_rates.T
    places = jnp.arange(span_len).astype(jnp.float32)
    block_items = (act_blocks, grad_blocks, inject_blocks, readout_blocks, rate_blocks)

    def forward_step(carried, members):
        block_act, block_grad, block_inject, block_readout, block_rates = members
        lead_decay = jnp.exp((places + 1.0)[:, None] * block_rates[None, :])
        tail_decay = jnp.exp((span_len - 1.0 - places)[:, None] * block_rates[None, :])
        inter_readout = jnp.einsum("qhp,hpn->qn", block_grad.astype(jnp.float32) * lead_decay[:, :, None], carried, precision=precise)
        fresh_state = jnp.einsum("qhp,qn->hpn", block_act.astype(jnp.float32) * tail_decay[:, :, None], block_inject.astype(jnp.float32), precision=precise)
        renewed = jnp.exp(span_len * block_rates)[:, None, None] * carried + fresh_state
        return renewed, inter_readout

    def backward_step(carried, members):
        block_act, block_grad, block_inject, block_readout, block_rates = members
        lead_decay = jnp.exp((places + 1.0)[:, None] * block_rates[None, :])
        outputs = span_terms(block_act, block_grad, block_inject, block_readout, block_rates, carried)
        fresh_grad = jnp.einsum("qhp,qn->hpn", block_grad.astype(jnp.float32) * lead_decay[:, :, None], block_readout.astype(jnp.float32), precision=precise)
        renewed = jnp.exp(span_len * block_rates)[:, None, None] * carried + fresh_grad
        return renewed, outputs

    empty_state = jnp.zeros((head_count, head_dim, states), jnp.float32)
    unused_state, inter_readout = lax.scan(forward_step, empty_state, block_items)
    unused_grad, outputs = lax.scan(backward_step, empty_state, block_items, reverse=True)
    grad_act, grad_inject, grad_readout = outputs
    grad_pre = grad_act.reshape(tokens, channels) * silu_slope(preact)
    padded_grad = jnp.concatenate([grad_pre, jnp.zeros((3, channels), jnp.float32)], axis=0)
    grad_input = weights[0] * padded_grad[3:3 + tokens]
    for offset in range(1, 4):
        grad_input = grad_input + weights[offset] * padded_grad[3 - offset:3 - offset + tokens]
    grad_readout = grad_readout + inter_readout
    return grad_input, grad_inject.reshape(tokens, states), grad_readout.reshape(tokens, states)
```

```python
import jax
import jax.numpy as jnp
from jax import lax
from jax.experimental import pallas as pl
from jax.experimental.pallas import tpu as pltpu
from jax.sharding import PartitionSpec as P

F32 = jnp.float32
BF16 = jnp.bfloat16
HALO = 16


def mm(a, b, ca, cb):
    return lax.dot_general(a, b, (((ca,), (cb,)), ((), ())), preferred_element_type=F32)


def chunks_of(channels):
    width = 128
    return [slice(i, i + width) for i in range(0, channels, width)]


def load_rows(first, x_ref, prev_ref, halo_ref, xs):
    span = x_ref.shape[0]

    @pl.when(first)
    def _():
        xs[0:HALO] = halo_ref[...].astype(F32)

    @pl.when(jnp.logical_not(first))
    def _():
        xs[0:HALO] = prev_ref[...].astype(F32)

    xs[HALO : HALO + span] = x_ref[...].astype(F32)


def preact_of(xs, w_ref, cols, span):
    v = w_ref[0:1, cols] * xs[HALO - 3 : HALO - 3 + span, cols]
    for k in range(1, 4):
        v = v + w_ref[k : k + 1, cols] * xs[HALO - 3 + k : HALO - 3 + k + span, cols]
    return v


def centred(span, width):
    rows = lax.broadcasted_iota(jnp.int32, (span, width), 0)
    return (rows - span // 2).astype(F32)


def fold_kernel(
    x_ref, prev_ref, halo_ref, g_ref, b_ref, c_ref, w_ref, lr_ref,
    before_ref, fresh_ref, own_state_ref, own_grad_ref,
    xs, act, da, dg, running,
):
    s = pl.program_id(0)
    span, channels = x_ref.shape
    load_rows(s == 0, x_ref, prev_ref, halo_ref, xs)

    @pl.when(s == 0)
    def _():
        own_state_ref[...] = jnp.zeros_like(own_state_ref)
        own_grad_ref[...] = jnp.zeros_like(own_grad_ref)
        running[...] = jnp.zeros_like(running)

    for cols in chunks_of(channels):
        v = preact_of(xs, w_ref, cols, span)
        a = (v * (1.0 / (1.0 + jnp.exp(-v)))).astype(BF16)
        act[:, cols] = a
        turn = centred(span, a.shape[1]) * lr_ref[0, 0:1, cols]
        da[:, cols] = (a.astype(F32) * (jnp.exp(-turn) - 1.0)).astype(BF16)
        dg[:, cols] = (g_ref[:, cols].astype(F32) * (jnp.exp(turn) - 1.0)).astype(BF16)
    lr = lr_ref[0]
    half = span // 2
    b, c = b_ref[...], c_ref[...]
    fresh_state = jnp.exp((half - 1.0) * lr) * (mm(b, act[...], 0, 0) + mm(b, da[...], 0, 0))
    fresh_grad = jnp.exp((half + 1.0) * lr) * (mm(c, g_ref[...], 0, 0) + mm(c, dg[...], 0, 0))
    before_ref[0] = own_state_ref[...]
    fresh_ref[0] = fresh_grad
    own_state_ref[...] = jnp.exp(span * lr) * own_state_ref[...] + fresh_state
    own_grad_ref[...] = own_grad_ref[...] + jnp.exp(running[0:1]) * fresh_grad
    running[...] = running[...] + span * lr


def grads_kernel(
    x_ref, prev_ref, halo_ref, g_ref, b_ref, c_ref, w_ref, lr_ref, prior_ref,
    before_ref, fresh_ref, entering_ref, arriving_ref,
    gx_ref, gb_ref, gc_ref, first_ref,
    xs, act, ab, gs, da, dg, sb_hi, sb_lo, ga_hi, ga_lo, gp, carry,
):
    t = pl.program_id(0)
    spans = pl.num_programs(0)
    span, channels = x_ref.shape
    half = span // 2
    load_rows(t == spans - 1, x_ref, prev_ref, halo_ref, xs)

    @pl.when(t == 0)
    def _():
        carry[...] = arriving_ref[...]
        gp[span : span + 8] = jnp.zeros((8, channels), F32)

    @pl.when(t > 0)
    def _():
        gp[span : span + 8] = gp[0:8]

    for cols in chunks_of(channels):
        lr = lr_ref[0, 0:1, cols]
        v = preact_of(xs, w_ref, cols, span)
        a = (v * (1.0 / (1.0 + jnp.exp(-v)))).astype(BF16)
        act[:, cols] = a
        turn = centred(span, a.shape[1]) * lr
        af = a.astype(F32)
        a_more = af * (jnp.exp(-turn) - 1.0)
        ab[:, cols] = (af + a_more).astype(BF16)
        da[:, cols] = a_more.astype(BF16)
        gf = g_ref[:, cols].astype(F32)
        g_more = gf * (jnp.exp(turn) - 1.0)
        gs[:, cols] = (gf + g_more).astype(BF16)
        dg[:, cols] = g_more.astype(BF16)
        held = carry[:, cols]
        sb = jnp.exp((half + 1.0) * lr) * (
            before_ref[0, :, cols] + prior_ref[0, 0:1, cols] * entering_ref[:, cols]
        )
        hi = sb.astype(BF16)
        sb_hi[:, cols] = hi
        sb_lo[:, cols] = (sb - hi.astype(F32)).astype(BF16)
        ga = jnp.exp((half - 1.0) * lr) * held
        hi = ga.astype(BF16)
        ga_hi[:, cols] = hi
        ga_lo[:, cols] = (ga - hi.astype(F32)).astype(BF16)
        carry[:, cols] = jnp.exp(span * lr) * held + fresh_ref[0, :, cols]

    b, c = b_ref[...], c_ref[...]
    rows = lax.broadcasted_iota(jnp.int32, (span, span), 0)
    columns = lax.broadcasted_iota(jnp.int32, (span, span), 1)
    lower = rows >= columns
    pairs = jnp.where(lower, mm(gs[...], ab[...], 1, 1), 0.0).astype(BF16)
    gb_ref[...] = (
        mm(pairs, c, 0, 0)
        + mm(act[...], ga_hi[...], 1, 1)
        + mm(act[...], ga_lo[...], 1, 1)
        + mm(da[...], ga_hi[...], 1, 1)
    )
    gc_ref[...] = (
        mm(pairs, b, 1, 0)
        + mm(g_ref[...], sb_hi[...], 1, 1)
        + mm(g_ref[...], sb_lo[...], 1, 1)
        + mm(dg[...], sb_hi[...], 1, 1)
    )
    mixed = jnp.where(lower, mm(c, b, 1, 1), 0.0).astype(BF16)

    for cols in chunks_of(channels):
        grad_act = mm(mixed, gs[:, cols], 0, 0) + mm(b, ga_hi[:, cols], 1, 0)
        grad_act = grad_act + mm(b, ga_lo[:, cols], 1, 0)
        v = preact_of(xs, w_ref, cols, span)
        squashed = 1.0 / (1.0 + jnp.exp(-v))
        slope = squashed * (1.0 + v * (1.0 - squashed))
        turn = centred(span, v.shape[1]) * lr_ref[0, 0:1, cols]
        gp[0:span, cols] = grad_act * jnp.exp(-turn) * slope
        out = w_ref[0:1, cols] * gp[3 : 3 + span, cols]
        for k in range(1, 4):
            out = out + w_ref[k : k + 1, cols] * gp[3 - k : 3 - k + span, cols]
        gx_ref[:, cols] = out
    first_ref[...] = gp[0:8]


def shifted(array, axis, by):
    length = lax.axis_size(axis)
    return lax.ppermute(
        array, axis, [(i, i + by) for i in range(length) if 0 <= i + by < length]
    )


def swapped(array, axis, flip):
    return lax.ppermute(array, axis, [(i, i ^ flip) for i in range(lax.axis_size(axis))])


def across_devices(own_state, own_grad, logs, head_dim):
    length, me = lax.axis_size("seq"), lax.axis_index("seq")
    places = jnp.arange(length)

    def gain(low, high):
        held = jnp.where(((places >= low) & (places <= high))[:, None], logs, 0.0)
        return jnp.repeat(jnp.exp(jnp.sum(held, axis=0)), head_dim)[None, :]

    entering, arriving = jnp.zeros_like(own_state), jnp.zeros_like(own_grad)
    state, grad = own_state, own_grad
    step = 1
    while step < length:
        got_state = shifted(state.astype(BF16), "seq", step).astype(F32)
        got_grad = shifted(grad.astype(BF16), "seq", -step).astype(F32)
        entering = entering + gain(me - step + 1, me - 1) * got_state
        arriving = arriving + gain(me + 1, me + step - 1) * got_grad
        if 2 * step < length:
            state = state + gain(me - step + 1, me) * got_state
            grad = grad + gain(me, me + step - 1) * got_grad
        step *= 2
    return entering, arriving


def summed_over_groups(both):
    length = lax.axis_size("hg")
    rows = both.shape[0] // 2
    odd = (lax.axis_index("hg") % 2) == 1
    low, high = both[:rows], both[rows:]
    mine = jnp.where(odd, high, low) + swapped(jnp.where(odd, low, high), "hg", 1)
    flip = 2
    while flip < length:
        sent = mine.astype(BF16)
        mine = sent.astype(F32) + swapped(sent, "hg", flip).astype(F32)
        flip *= 2
    other = swapped(mine, "hg", 1)
    return jnp.concatenate([jnp.where(odd, other, mine), jnp.where(odd, mine, other)], axis=0)


def body(conv_input, grad_output, inject, readout, conv_weight, decay_codes):
    tokens, channels = conv_input.shape
    heads, spans = decay_codes.shape
    span = tokens // spans
    head_dim = channels // heads
    states = inject.shape[1]
    weights = conv_weight.astype(F32)
    log_rates = jnp.log1p(-decay_codes.astype(F32) * 1e-06)
    own_logs = span * jnp.sum(log_rates, axis=1)
    logs = lax.all_gather(own_logs, "seq", axis=0)
    halo = shifted(conv_input[tokens - HALO :], "seq", 1)
    wide = jnp.repeat(log_rates.T, head_dim, axis=1)
    prior = jnp.exp(span * (jnp.cumsum(wide, axis=0) - wide))[:, None]
    lr = wide[:, None]
    step = span // HALO

    def specs(at):
        return [
            pl.BlockSpec((span, channels), lambda t: (at(t), 0)),
            pl.BlockSpec((HALO, channels), lambda t: (jnp.maximum(at(t) * step - 1, 0), 0)),
            pl.BlockSpec((HALO, channels), lambda t: (0, 0)),
            pl.BlockSpec((span, channels), lambda t: (at(t), 0)),
            pl.BlockSpec((span, states), lambda t: (at(t), 0)),
            pl.BlockSpec((span, states), lambda t: (at(t), 0)),
            pl.BlockSpec((4, channels), lambda t: (0, 0)),
            pl.BlockSpec((1, 1, channels), lambda t: (at(t), 0, 0)),
        ]

    per_span = jax.ShapeDtypeStruct((spans, states, channels), F32)
    one = jax.ShapeDtypeStruct((states, channels), F32)
    params = pltpu.CompilerParams(
        vmem_limit_bytes=48 << 20, dimension_semantics=("arbitrary",)
    )
    whole = pl.BlockSpec((states, channels), lambda t: (0, 0))
    lines = pltpu.VMEM((span + HALO, channels), F32)
    tile = pltpu.VMEM((span, channels), BF16)
    before, fresh, own_state, own_grad = pl.pallas_call(
        fold_kernel,
        grid=(spans,),
        in_specs=specs(lambda t: t),
        out_specs=[pl.BlockSpec((1, states, channels), lambda t: (t, 0, 0))] * 2 + [whole] * 2,
        out_shape=[per_span, per_span, one, one],
        scratch_shapes=[lines, tile, tile, tile, pltpu.VMEM((8, channels), F32)],
        compiler_params=params,
        name="fold",
    )(conv_input, conv_input, halo, grad_output, inject, readout, weights, lr)

    entering, arriving = across_devices(own_state, own_grad, logs, head_dim)

    back = lambda t: spans - 1 - t
    state_tile = pltpu.VMEM((states, channels), BF16)
    grad_input, grad_inject, grad_readout, first = pl.pallas_call(
        grads_kernel,
        grid=(spans,),
        in_specs=specs(back)
        + [pl.BlockSpec((1, 1, channels), lambda t: (back(t), 0, 0))]
        + [pl.BlockSpec((1, states, channels), lambda t: (back(t), 0, 0))] * 2
        + [whole] * 2,
        out_specs=[
            pl.BlockSpec((span, channels), lambda t: (back(t), 0)),
            pl.BlockSpec((span, states), lambda t: (back(t), 0)),
            pl.BlockSpec((span, states), lambda t: (back(t), 0)),
            pl.BlockSpec((8, channels), lambda t: (0, 0)),
        ],
        out_shape=[
            jax.ShapeDtypeStruct((tokens, channels), F32),
            jax.ShapeDtypeStruct((tokens, states), F32),
            jax.ShapeDtypeStruct((tokens, states), F32),
            jax.ShapeDtypeStruct((8, channels), F32),
        ],
        scratch_shapes=[lines]
        + [tile] * 5
        + [state_tile] * 4
        + [pltpu.VMEM((span + 8, channels), F32), pltpu.VMEM((states, channels), F32)],
        compiler_params=params,
        name="grads",
    )(
        conv_input, conv_input, halo, grad_output, inject, readout, weights, lr, prior,
        before, fresh, entering, arriving,
    )
    later = shifted(first, "seq", -1)
    edge = jnp.stack(
        [sum(weights[k] * later[r - k] for k in range(r + 1)) for r in range(3)], axis=0
    )
    last = grad_input[tokens - 8 :] + jnp.pad(edge, ((5, 0), (0, 0)))
    grad_input = lax.dynamic_update_slice(grad_input, last, (tokens - 8, 0))
    both = summed_over_groups(jnp.concatenate([grad_inject, grad_readout], axis=1))
    return grad_input, both[:, :states], both[:, states:]


def solution(mesh):
    return jax.shard_map(
        body,
        mesh=mesh,
        in_specs=(
            P("seq", "hg"),
            P("seq", "hg"),
            P("seq", None),
            P("seq", None),
            P(None, "hg"),
            P("hg", "seq"),
        ),
        out_specs=(P("seq", "hg"), P("seq", None), P("seq", None)),
        check_vma=False,
    )
```

```python
import functools

import jax
import jax.numpy as jnp
from jax import lax
from jax.experimental import pallas as pl
from jax.experimental.pallas import tpu as pltpu
from jax.sharding import PartitionSpec as P

F32 = jnp.float32
BF16 = jnp.bfloat16
HALO = 16


def mm(a, b, ca, cb):
    return lax.dot_general(a, b, (((ca,), (cb,)), ((), ())), preferred_element_type=F32)


def chunks_of(channels):
    width = 256
    return [slice(i, i + width) for i in range(0, channels, width)]


def load_rows(first, x_ref, prev_ref, halo_ref, xs):
    span = x_ref.shape[0]

    @pl.when(first)
    def _():
        xs[0:HALO] = halo_ref[...].astype(F32)

    @pl.when(jnp.logical_not(first))
    def _():
        xs[0:HALO] = prev_ref[...].astype(F32)

    xs[HALO : HALO + span] = x_ref[...].astype(F32)


def preact_of(xs, w_ref, cols, span):
    v = w_ref[0:1, cols] * xs[HALO - 3 : HALO - 3 + span, cols]
    for k in range(1, 4):
        v = v + w_ref[k : k + 1, cols] * xs[HALO - 3 + k : HALO - 3 + k + span, cols]
    return v


def decays(lr, span):
    width = lr.shape[1]
    rows = lax.broadcasted_iota(jnp.int32, (8, width), 0)
    held = jnp.exp((rows - span // 2).astype(F32) * lr)
    length = 8
    while length < span:
        held = jnp.concatenate([held, held * jnp.exp(length * lr)], axis=0)
        length *= 2
    return held


def fold_kernel(
    x_ref, prev_ref, halo_ref, g_ref, b_ref, c_ref, w_ref, lr_ref,
    act_ref, da_ref, dg_ref, slope_ref, before_ref, fresh_ref, own_state_ref, own_grad_ref,
    xs, running,
):
    s = pl.program_id(0)
    span, channels = x_ref.shape
    half = span // 2
    load_rows(s == 0, x_ref, prev_ref, halo_ref, xs)

    @pl.when(s == 0)
    def _():
        own_state_ref[...] = jnp.zeros_like(own_state_ref)
        own_grad_ref[...] = jnp.zeros_like(own_grad_ref)
        running[...] = jnp.zeros_like(running)

    b, c = b_ref[...].T, c_ref[...].T
    for cols in chunks_of(channels):
        lr = lr_ref[0, 0:1, cols]
        v = preact_of(xs, w_ref, cols, span)
        squashed = 0.5 + 0.5 * jnp.tanh(0.5 * v)
        full = v * squashed
        slope_ref[:, cols] = (squashed + full * (1.0 - squashed) - 0.5).astype(BF16)
        a = full.astype(BF16)
        act_ref[:, cols] = a
        da = (a.astype(F32) * (decays(-lr, span) - 1.0)).astype(BF16)
        da_ref[:, cols] = da
        g = g_ref[:, cols]
        dg = (g.astype(F32) * (decays(lr, span) - 1.0)).astype(BF16)
        dg_ref[:, cols] = dg
        fresh_state = jnp.exp((half - 1.0) * lr) * (mm(b, a, 1, 0) + mm(b, da, 1, 0))
        fresh_grad = jnp.exp((half + 1.0) * lr) * (mm(c, g, 1, 0) + mm(c, dg, 1, 0))
        held = own_state_ref[:, cols]
        before_ref[0, :, cols] = held
        fresh_ref[0, :, cols] = fresh_grad
        own_state_ref[:, cols] = jnp.exp(span * lr) * held + fresh_state
        own_grad_ref[:, cols] = own_grad_ref[:, cols] + jnp.exp(running[0:1, cols]) * fresh_grad
    running[...] = running[...] + span * lr_ref[0]


def log_rows(log):
    high = log.astype(BF16).astype(F32)
    mid = (log - high).astype(BF16).astype(F32)
    low = log - high - mid
    rows = lax.broadcasted_iota(jnp.int32, (HALO, log.shape[1]), 0)
    tile = jnp.where(rows == 0, high, jnp.where(rows == 1, mid, jnp.where(rows == 2, low, 0.0)))
    return tile.astype(BF16)


def inner_kernel(
    length, rounds, axis,
    g_ref, dg_ref, act_ref, da_ref, b_ref, c_ref, own_state_ref, own_grad_ref, log_ref,
    ga_ref, gb_ref, gc_ref, entering_ref, arriving_ref,
    sent, landed, held, logs, send_sem, recv_sem,
):
    t = pl.program_id(0)
    spans = pl.num_programs(0)
    span = b_ref.shape[0]
    size = own_state_ref.shape[0]
    me = lax.axis_index(axis)
    founds = (entering_ref, arriving_ref)

    def inside(device):
        return jnp.logical_and(device >= 0, device < length)

    def copy(way, r):
        by = (1 << r) * (1 - 2 * way)
        move = pltpu.make_async_remote_copy(
            src_ref=sent.at[way, r],
            dst_ref=landed.at[way, r],
            send_sem=send_sem.at[way, r],
            recv_sem=recv_sem.at[way, r],
            device_id={axis: me + by},
            device_id_type=pl.DeviceIdType.MESH,
        )
        return move, inside(me + by), inside(me - by)

    def start(r):
        for way in range(2):
            sent[way, r, 0:size] = held[way].astype(BF16)
            sent[way, r, size : size + HALO] = log_rows(logs[way, 0:1])
            move, sends, _ = copy(way, r)

            @pl.when(sends)
            def _():
                move.start()

    def finish(r):
        for way in range(2):
            move, sends, takes = copy(way, r)

            @pl.when(takes)
            def _():
                move.wait_recv()
                got = landed[way, r, 0:size].astype(F32)
                tail = landed[way, r, size : size + HALO].astype(F32)
                got_log = (tail[0:1] + tail[1:2]) + tail[2:3]
                found = founds[way]
                found[...] = found[...] + jnp.exp(logs[way, 1:2]) * got
                if r < rounds - 1:
                    held[way] = held[way] + jnp.exp(logs[way, 0:1]) * got
                    logs[way, 0:1] = logs[way, 0:1] + got_log
                    logs[way, 1:2] = logs[way, 1:2] + got_log

            @pl.when(sends)
            def _():
                move.wait_send()

    @pl.when(t == 0)
    def _():
        barrier = pltpu.get_barrier_semaphore()
        others = [me + sign * (1 << r) for r in range(rounds) for sign in (1, -1)]
        for other in others:

            @pl.when(inside(other))
            def _():
                pl.semaphore_signal(
                    barrier, inc=1, device_id={axis: other}, device_id_type=pl.DeviceIdType.MESH
                )

        pl.semaphore_wait(barrier, sum(jnp.where(inside(other), 1, 0) for other in others))

        for way, (own, found) in enumerate(zip((own_state_ref, own_grad_ref), founds)):
            held[way] = own[...]
            logs[way, 0:1] = log_ref[...]
            logs[way, 1:2] = jnp.zeros_like(log_ref)
            found[...] = jnp.zeros_like(found)

    for r in range(rounds):

        @pl.when(t == r * spans // rounds)
        def _():
            if r > 0:
                finish(r - 1)
            start(r)

    b, c = b_ref[...], c_ref[...]
    rows = lax.broadcasted_iota(jnp.int32, (span, span), 0)
    columns = lax.broadcasted_iota(jnp.int32, (span, span), 1)
    mixed = jnp.where(rows <= columns, mm(b, c, 1, 1), 0.0).astype(BF16)
    pairs = jnp.zeros((span, span), F32)
    for cols in chunks_of(g_ref.shape[1]):
        gs = (g_ref[:, cols].astype(F32) + dg_ref[:, cols].astype(F32)).astype(BF16)
        ab = (act_ref[:, cols].astype(F32) + da_ref[:, cols].astype(F32)).astype(BF16)
        pairs = pairs + mm(gs, ab, 1, 1)
        ga_ref[:, cols] = mm(mixed, gs, 1, 0).astype(BF16)
    pairs = jnp.where(rows >= columns, pairs, 0.0).astype(BF16)
    gb_ref[...] = mm(pairs, c, 0, 0)
    gc_ref[...] = mm(pairs, b, 1, 0)

    @pl.when(t == spans - 1)
    def _():
        finish(rounds - 1)


def quadrants(high_ref, low_ref, pair):
    span, size = high_ref.shape[0], pair.shape[0] // 2
    stacked = jnp.concatenate([high_ref[...], low_ref[...]], axis=0)
    products = mm(stacked, pair, 1, 1)
    rows = products[:span] + products[span:]
    return rows[:, :size] + rows[:, size:]


def shared_kernel(
    g_ref, dg_ref, act_ref, da_ref, lr_ref, prior_ref, before_ref, fresh_ref,
    entering_ref, arriving_ref, inner_b_ref, inner_c_ref,
    pair_ref, both_ref, states, carry,
):
    t = pl.program_id(0)
    span, channels = g_ref.shape
    half = span // 2
    size = carry.shape[0]

    @pl.when(t == 0)
    def _():
        carry[...] = arriving_ref[...]

    for cols in chunks_of(channels):
        lr = lr_ref[0, 0:1, cols]
        sb = jnp.exp((half + 1.0) * lr) * (
            before_ref[0, :, cols] + prior_ref[0, 0:1, cols] * entering_ref[:, cols]
        )
        hi = sb.astype(BF16)
        states[0:size, cols] = hi
        states[size : 2 * size, cols] = (sb - hi.astype(F32)).astype(BF16)
        held = carry[:, cols]
        ga = jnp.exp((half - 1.0) * lr) * held
        hi = ga.astype(BF16)
        pair_ref[0, 0:size, cols] = hi
        pair_ref[0, size : 2 * size, cols] = (ga - hi.astype(F32)).astype(BF16)
        carry[:, cols] = jnp.exp(span * lr) * held + fresh_ref[0, :, cols]
    both_ref[:, 0:size] = inner_b_ref[...] + quadrants(act_ref, da_ref, pair_ref[0])
    both_ref[:, size:] = inner_c_ref[...] + quadrants(g_ref, dg_ref, states[...])


def input_kernel(
    b_ref, w_ref, lr_ref, pair_ref, ga_ref, slope_ref,
    gx_ref, first_ref, gp,
):
    t = pl.program_id(0)
    span, channels = ga_ref.shape

    @pl.when(t == 0)
    def _():
        gp[span : span + 8] = jnp.zeros((8, channels), F32)

    @pl.when(t > 0)
    def _():
        gp[span : span + 8] = gp[0:8]

    twice = jnp.concatenate([b_ref[...], b_ref[...]], axis=1)
    for cols in chunks_of(channels):
        grad_act = mm(twice, pair_ref[0, :, cols], 1, 0) + ga_ref[:, cols].astype(F32)
        slope = slope_ref[:, cols].astype(F32) + 0.5
        gp[0:span, cols] = grad_act * decays(-lr_ref[0, 0:1, cols], span) * slope
        out = w_ref[0:1, cols] * gp[3 : 3 + span, cols]
        for k in range(1, 4):
            out = out + w_ref[k : k + 1, cols] * gp[3 - k : 3 - k + span, cols]
        gx_ref[:, cols] = out
    first_ref[...] = gp[0:8]


def shifted(array, axis, by):
    length = lax.axis_size(axis)
    return lax.ppermute(
        array, axis, [(i, i + by) for i in range(length) if 0 <= i + by < length]
    )


def swapped(array, axis, flip):
    return lax.ppermute(array, axis, [(i, i ^ flip) for i in range(lax.axis_size(axis))])


def half_sums(both):
    rows = both.shape[0] // 2
    odd = (lax.axis_index("hg") % 2) == 1
    low, high = both[:rows], both[rows:]
    return jnp.where(odd, high, low) + swapped(jnp.where(odd, low, high), "hg", 1)


def pair_sums(mine):
    flip = 2
    while flip < lax.axis_size("hg"):
        sent = mine.astype(BF16)
        mine = sent.astype(F32) + swapped(sent, "hg", flip).astype(F32)
        flip *= 2
    return mine


def joined_halves(mine):
    odd = (lax.axis_index("hg") % 2) == 1
    other = swapped(mine, "hg", 1)
    return jnp.concatenate([jnp.where(odd, other, mine), jnp.where(odd, mine, other)], axis=0)


def body(conv_input, grad_output, inject, readout, conv_weight, decay_codes):
    tokens, channels = conv_input.shape
    heads, spans = decay_codes.shape
    span = tokens // spans
    head_dim = channels // heads
    states = inject.shape[1]
    weights = conv_weight.astype(F32)
    log_rates = jnp.log1p(-decay_codes.astype(F32) * 1e-06)
    halo = shifted(conv_input[tokens - HALO :], "seq", 1)
    wide = jnp.repeat(log_rates.T, head_dim, axis=1)
    prior = jnp.exp(span * (jnp.cumsum(wide, axis=0) - wide))[:, None]
    own_log = span * jnp.sum(wide, axis=0, keepdims=True)
    lr = wide[:, None]
    step = span // HALO
    params = pltpu.CompilerParams(
        vmem_limit_bytes=48 << 20, dimension_semantics=("arbitrary",)
    )
    on = lambda t: t
    back = lambda t: spans - 1 - t

    def tile(at, width):
        return pl.BlockSpec((span, width), lambda t: (at(t), 0))

    def block(at, rows, width):
        return pl.BlockSpec((1, rows, width), lambda t: (at(t), 0, 0))

    def fixed(rows):
        return pl.BlockSpec((rows, channels), lambda t: (0, 0))

    def like(shape, dtype):
        return jax.ShapeDtypeStruct(shape, dtype)

    def cost(products, moved):
        return pl.CostEstimate(
            flops=2 * products * tokens * channels, bytes_accessed=moved, transcendentals=0
        )

    size = tokens * channels
    wide_tokens = like((tokens, channels), BF16)
    act, da, dg, slope, before, fresh, own_state, own_grad = pl.pallas_call(
        fold_kernel,
        grid=(spans,),
        in_specs=[
            tile(on, channels),
            pl.BlockSpec((HALO, channels), lambda t: (jnp.maximum(t * step - 1, 0), 0)),
            fixed(HALO),
            tile(on, channels),
            tile(on, states),
            tile(on, states),
            fixed(4),
            block(on, 1, channels),
        ],
        out_specs=[tile(on, channels)] * 4
        + [block(on, states, channels)] * 2
        + [fixed(states)] * 2,
        out_shape=[wide_tokens] * 4
        + [like((spans, states, channels), F32)] * 2
        + [like((states, channels), F32)] * 2,
        scratch_shapes=[
            pltpu.VMEM((span + HALO, channels), F32),
            pltpu.VMEM((8, channels), F32),
        ],
        compiler_params=params,
        cost_estimate=cost(4 * states, 16 * size),
        name="fold",
    )(conv_input, conv_input, halo, grad_output, inject, readout, weights, lr)

    length = lax.axis_size("seq")
    rounds = (length - 1).bit_length()
    inner_act, inner_b, inner_c, entering, arriving = pl.pallas_call(
        functools.partial(inner_kernel, length, rounds, "seq"),
        grid=(spans,),
        in_specs=[tile(on, channels)] * 4
        + [tile(on, states)] * 2
        + [fixed(states)] * 2
        + [fixed(1)],
        out_specs=[tile(on, channels)] + [tile(on, states)] * 2 + [fixed(states)] * 2,
        out_shape=[wide_tokens]
        + [like((tokens, states), F32)] * 2
        + [like((states, channels), F32)] * 2,
        scratch_shapes=[
            pltpu.VMEM((2, rounds, states + HALO, channels), BF16),
            pltpu.VMEM((2, rounds, states + HALO, channels), BF16),
            pltpu.VMEM((2, states, channels), F32),
            pltpu.VMEM((2, 8, channels), F32),
            pltpu.SemaphoreType.DMA((2, rounds)),
            pltpu.SemaphoreType.DMA((2, rounds)),
        ],
        compiler_params=pltpu.CompilerParams(
            vmem_limit_bytes=48 << 20,
            dimension_semantics=("arbitrary",),
            collective_id=0,
            has_side_effects=True,
        ),
        cost_estimate=cost(2 * span + states, 10 * size),
        name="inner",
    )(grad_output, dg, act, da, inject, readout, own_state, own_grad, own_log)
    pairs, both = pl.pallas_call(
        shared_kernel,
        grid=(spans,),
        in_specs=[tile(back, channels)] * 4
        + [block(back, 1, channels)] * 2
        + [block(back, states, channels)] * 2
        + [fixed(states)] * 2
        + [tile(back, states)] * 2,
        out_specs=[block(back, 2 * states, channels), tile(back, 2 * states)],
        out_shape=[
            like((spans, 2 * states, channels), BF16),
            like((tokens, 2 * states), F32),
        ],
        scratch_shapes=[
            pltpu.VMEM((2 * states, channels), BF16),
            pltpu.VMEM((states, channels), F32),
        ],
        compiler_params=params,
        cost_estimate=cost(8 * states, 14 * size),
        name="shared",
    )(grad_output, dg, act, da, lr, prior, before, fresh, entering, arriving, inner_b, inner_c)

    mine, pairs = lax.optimization_barrier((half_sums(both), pairs))
    grad_input, first = pl.pallas_call(
        input_kernel,
        grid=(spans,),
        in_specs=[
            tile(back, states),
            fixed(4),
            block(back, 1, channels),
            block(back, 2 * states, channels),
            tile(back, channels),
            tile(back, channels),
        ],
        out_specs=[tile(back, channels), fixed(8)],
        out_shape=[like((tokens, channels), F32), like((8, channels), F32)],
        scratch_shapes=[pltpu.VMEM((span + 8, channels), F32)],
        compiler_params=params,
        cost_estimate=cost(2 * states, 10 * size),
        name="inputs",
    )(inject, weights, lr, pairs, inner_act, slope)
    mine, first = lax.optimization_barrier((pair_sums(mine), first))
    later = shifted(first, "seq", -1)
    edge = jnp.stack(
        [sum(weights[k] * later[r - k] for k in range(r + 1)) for r in range(3)], axis=0
    )
    last = grad_input[tokens - 8 :] + jnp.pad(edge, ((5, 0), (0, 0)))
    grad_input = lax.dynamic_update_slice(grad_input, last, (tokens - 8, 0))
    total = joined_halves(mine)
    return grad_input, total[:, :states], total[:, states:]


def solution(mesh):
    return jax.shard_map(
        body,
        mesh=mesh,
        in_specs=(
            P("seq", "hg"),
            P("seq", "hg"),
            P("seq", None),
            P("seq", None),
            P(None, "hg"),
            P("hg", "seq"),
        ),
        out_specs=(P("seq", "hg"), P("seq", None), P("seq", None)),
        check_vma=False,
    )
```

```python
import functools

import jax
import jax.numpy as jnp
from jax import lax
from jax.experimental import pallas as pl
from jax.experimental.pallas import tpu as pltpu
from jax.sharding import PartitionSpec as P

F32 = jnp.float32
BF16 = jnp.bfloat16
HALO = 16


def mm(a, b, ca, cb):
    return lax.dot_general(a, b, (((ca,), (cb,)), ((), ())), preferred_element_type=F32)


WIDTH = 256


def chunks_of(channels):
    return [slice(i, i + WIDTH) for i in range(0, channels, WIDTH)]


def preact_of(xs, w_ref, at, span):
    v = w_ref[0:1] * xs[at + HALO - 3 : at + HALO - 3 + span]
    for k in range(1, 4):
        v = v + w_ref[k : k + 1] * xs[at + HALO - 3 + k : at + HALO - 3 + k + span]
    return v


def decays(lr, span):
    width = lr.shape[1]
    rows = lax.broadcasted_iota(jnp.int32, (8, width), 0)
    held = jnp.exp((rows - span // 2).astype(F32) * lr)
    length = 8
    while length < span:
        held = jnp.concatenate([held, held * jnp.exp(length * lr)], axis=0)
        length *= 2
    return held


def log_rows(log):
    high = log.astype(BF16).astype(F32)
    mid = (log - high).astype(BF16).astype(F32)
    low = log - high - mid
    rows = lax.broadcasted_iota(jnp.int32, (HALO, log.shape[1]), 0)
    tile = jnp.where(rows == 0, high, jnp.where(rows == 1, mid, jnp.where(rows == 2, low, 0.0)))
    return tile.astype(BF16)


def fold_kernel(
    length, rounds, axis, span,
    x_ref, prev_ref, halo_ref, g_ref, b_ref, c_ref, w_ref, lr_ref, log_ref,
    act_ref, da_ref, dg_ref, slope_ref, before_ref, fresh_ref,
    ga_ref, gb_ref, gc_ref, entering_ref, arriving_ref,
    xs, gs, ab, running, held, logs, sent, landed, send_sem, recv_sem,
):
    t = pl.program_id(0)
    chunks, size = held.shape[1], held.shape[2]
    rows, width = x_ref.shape
    parts = b_ref.shape[0] // rows
    spans = b_ref.shape[0] // span
    folding = chunks * parts
    half = span // 2
    me = lax.axis_index(axis)
    founds = (entering_ref, arriving_ref)

    def inside(device):
        return jnp.logical_and(device >= 0, device < length)

    def copy(way, n, r):
        by = (1 << r) * (1 - 2 * way)
        move = pltpu.make_async_remote_copy(
            src_ref=sent.at[way, n, r],
            dst_ref=landed.at[way, n, r],
            send_sem=send_sem.at[way, n, r],
            recv_sem=recv_sem.at[way, n, r],
            device_id={axis: me + by},
            device_id_type=pl.DeviceIdType.MESH,
        )
        return move, inside(me + by), inside(me - by)

    def start(n, r):
        for way in range(2):
            sent[way, n, r, 0:size] = held[way, n].astype(BF16)
            sent[way, n, r, size : size + HALO] = log_rows(logs[way, n, 0:1])
            move, sends, _ = copy(way, n, r)

            @pl.when(sends)
            def _():
                move.start()

    def finish(n, r):
        for way in range(2):
            move, sends, takes = copy(way, n, r)

            @pl.when(takes)
            def _():
                move.wait_recv()
                got = landed[way, n, r, 0:size].astype(F32)
                tail = landed[way, n, r, size : size + HALO].astype(F32)
                got_log = (tail[0:1] + tail[1:2]) + tail[2:3]
                found = founds[way]
                found[n] = found[n] + jnp.exp(logs[way, n, 1:2]) * got
                if r < rounds - 1:
                    held[way, n] = held[way, n] + jnp.exp(logs[way, n, 0:1]) * got
                    logs[way, n, 0:1] = logs[way, n, 0:1] + got_log
                    logs[way, n, 1:2] = logs[way, n, 1:2] + got_log

            @pl.when(sends)
            def _():
                move.wait_send()

    @pl.when(t == 0)
    def _():
        barrier = pltpu.get_barrier_semaphore()
        others = [me + sign * (1 << r) for r in range(rounds) for sign in (1, -1)]
        for other in others:

            @pl.when(inside(other))
            def _():
                pl.semaphore_signal(
                    barrier, inc=1, device_id={axis: other}, device_id_type=pl.DeviceIdType.MESH
                )

        pl.semaphore_wait(barrier, sum(jnp.where(inside(other), 1, 0) for other in others))
        held[...] = jnp.zeros_like(held)
        for way, found in enumerate(founds):
            found[...] = jnp.zeros_like(found)
            for n in range(chunks):
                logs[way, n, 0:1] = log_ref[n]
                logs[way, n, 1:2] = jnp.zeros((1, width), F32)

    @pl.when(t < folding)
    def _():
        n, part = t // parts, t % parts

        @pl.when(part == 0)
        def _():
            xs[0:HALO] = halo_ref[...].astype(F32)
            running[...] = jnp.zeros_like(running)

        @pl.when(part > 0)
        def _():
            xs[0:HALO] = prev_ref[...].astype(F32)

        xs[HALO : HALO + rows] = x_ref[...].astype(F32)
        for q in range(rows // span):
            at = q * span
            here = slice(at, at + span)
            place = pl.multiple_of(part * rows + at, span)
            lr = lr_ref[pl.ds(part * (rows // span) + q, 1)]
            b = b_ref[pl.ds(place, span)].T
            c = c_ref[pl.ds(place, span)].T
            v = preact_of(xs, w_ref, at, span)
            squashed = 0.5 + 0.5 * jnp.tanh(0.5 * v)
            full = v * squashed
            slope_ref[here] = (squashed + full * (1.0 - squashed) - 0.5).astype(BF16)
            a = full.astype(BF16)
            act_ref[here] = a
            af = a.astype(F32)
            more = af * (decays(-lr, span) - 1.0)
            da = more.astype(BF16)
            da_ref[here] = da
            ab[n, pl.ds(place, span)] = (af + more).astype(BF16)
            g = g_ref[here]
            gf = g.astype(F32)
            more = gf * (decays(lr, span) - 1.0)
            dg = more.astype(BF16)
            dg_ref[here] = dg
            gs[n, pl.ds(place, span)] = (gf + more).astype(BF16)
            fresh_state = jnp.exp((half - 1.0) * lr) * (mm(b, a, 1, 0) + mm(b, da, 1, 0))
            fresh_grad = jnp.exp((half + 1.0) * lr) * (mm(c, g, 1, 0) + mm(c, dg, 1, 0))
            state = held[0, n]
            before_ref[q] = state
            fresh_ref[q] = fresh_grad
            held[0, n] = jnp.exp(span * lr) * state + fresh_state
            held[1, n] = held[1, n] + jnp.exp(running[0:1]) * fresh_grad
            running[...] = running[...] + span * lr

    @pl.when(t >= folding)
    def _():
        place = pl.multiple_of((t - folding) * span, span)
        b, c = b_ref[pl.ds(place, span)], c_ref[pl.ds(place, span)]
        down = lax.broadcasted_iota(jnp.int32, (span, span), 0)
        along = lax.broadcasted_iota(jnp.int32, (span, span), 1)
        mixed = jnp.where(down <= along, mm(b, c, 1, 1), 0.0).astype(BF16)
        pairs = jnp.zeros((span, span), F32)
        for n in range(chunks):
            scaled = gs[n, pl.ds(place, span)]
            pairs = pairs + mm(scaled, ab[n, pl.ds(place, span)], 1, 1)
            ga_ref[:, n * width : (n + 1) * width] = mm(mixed, scaled, 1, 0).astype(BF16)
        pairs = jnp.where(down >= along, pairs, 0.0).astype(BF16)
        gb_ref[...] = mm(pairs, c, 0, 0)
        gc_ref[...] = mm(pairs, b, 1, 0)

    def step_of(n, r):
        step = parts * (n + 1) - 1 + 2 * r
        over = step - (folding - 1)
        return step if over <= 0 else folding - 1 + over * spans // (2 * rounds)

    for n in range(chunks):
        for r in range(rounds + 1):

            @pl.when(t == step_of(n, r))
            def _():
                if r > 0:
                    finish(n, r - 1)
                if r < rounds:
                    start(n, r)


def quadrants(high_ref, low_ref, pair):
    span, size = high_ref.shape[0], pair.shape[0] // 2
    stacked = jnp.concatenate([high_ref[...], low_ref[...]], axis=0)
    products = mm(stacked, pair, 1, 1)
    rows = products[:span] + products[span:]
    return rows[:, :size] + rows[:, size:]


def shared_kernel(
    g_ref, dg_ref, act_ref, da_ref, lr_ref, prior_ref, before_ref, fresh_ref,
    entering_ref, arriving_ref, inner_b_ref, inner_c_ref,
    pair_ref, both_ref, states, carry,
):
    t = pl.program_id(0)
    span, channels = g_ref.shape
    half = span // 2
    size = carry.shape[0]

    @pl.when(t == 0)
    def _():
        for n, cols in enumerate(chunks_of(channels)):
            carry[:, cols] = arriving_ref[n]

    for n, cols in enumerate(chunks_of(channels)):
        lr = lr_ref[0, 0:1, cols]
        sb = jnp.exp((half + 1.0) * lr) * (
            before_ref[0, :, cols] + prior_ref[0, 0:1, cols] * entering_ref[n]
        )
        hi = sb.astype(BF16)
        states[0:size, cols] = hi
        states[size : 2 * size, cols] = (sb - hi.astype(F32)).astype(BF16)
        held = carry[:, cols]
        ga = jnp.exp((half - 1.0) * lr) * held
        hi = ga.astype(BF16)
        pair_ref[0, 0:size, cols] = hi
        pair_ref[0, size : 2 * size, cols] = (ga - hi.astype(F32)).astype(BF16)
        carry[:, cols] = jnp.exp(span * lr) * held + fresh_ref[0, :, cols]
    both_ref[:, 0:size] = inner_b_ref[...] + quadrants(act_ref, da_ref, pair_ref[0])
    both_ref[:, size:] = inner_c_ref[...] + quadrants(g_ref, dg_ref, states[...])


def input_kernel(
    b_ref, w_ref, lr_ref, pair_ref, ga_ref, slope_ref,
    gx_ref, first_ref, gp,
):
    t = pl.program_id(0)
    span, channels = ga_ref.shape

    @pl.when(t == 0)
    def _():
        gp[span : span + 8] = jnp.zeros((8, channels), F32)

    @pl.when(t > 0)
    def _():
        gp[span : span + 8] = gp[0:8]

    twice = jnp.concatenate([b_ref[...], b_ref[...]], axis=1)
    for cols in chunks_of(channels):
        grad_act = mm(twice, pair_ref[0, :, cols], 1, 0) + ga_ref[:, cols].astype(F32)
        slope = slope_ref[:, cols].astype(F32) + 0.5
        gp[0:span, cols] = grad_act * decays(-lr_ref[0, 0:1, cols], span) * slope
        out = w_ref[0:1, cols] * gp[3 : 3 + span, cols]
        for k in range(1, 4):
            out = out + w_ref[k : k + 1, cols] * gp[3 - k : 3 - k + span, cols]
        gx_ref[:, cols] = out
    first_ref[...] = gp[0:8]


def shifted(array, axis, by):
    length = lax.axis_size(axis)
    return lax.ppermute(
        array, axis, [(i, i + by) for i in range(length) if 0 <= i + by < length]
    )


def swapped(array, axis, flip):
    return lax.ppermute(array, axis, [(i, i ^ flip) for i in range(lax.axis_size(axis))])


def half_sums(both):
    rows = both.shape[0] // 2
    odd = (lax.axis_index("hg") % 2) == 1
    low, high = both[:rows], both[rows:]
    return jnp.where(odd, high, low) + swapped(jnp.where(odd, low, high), "hg", 1)


def pair_sums(mine):
    flip = 2
    while flip < lax.axis_size("hg"):
        sent = mine.astype(BF16)
        mine = sent.astype(F32) + swapped(sent, "hg", flip).astype(F32)
        flip *= 2
    return mine


def joined_halves(mine):
    odd = (lax.axis_index("hg") % 2) == 1
    other = swapped(mine, "hg", 1)
    return jnp.concatenate([jnp.where(odd, other, mine), jnp.where(odd, mine, other)], axis=0)


def body(conv_input, grad_output, inject, readout, conv_weight, decay_codes):
    tokens, channels = conv_input.shape
    heads, spans = decay_codes.shape
    span = tokens // spans
    head_dim = channels // heads
    states = inject.shape[1]
    weights = conv_weight.astype(F32)
    log_rates = jnp.log1p(-decay_codes.astype(F32) * 1e-06)
    halo = shifted(conv_input[tokens - HALO :], "seq", 1)
    wide = jnp.repeat(log_rates.T, head_dim, axis=1)
    prior = jnp.exp(span * (jnp.cumsum(wide, axis=0) - wide))[:, None]
    own_log = span * jnp.sum(wide, axis=0, keepdims=True)
    lr = wide[:, None]
    params = pltpu.CompilerParams(
        vmem_limit_bytes=48 << 20, dimension_semantics=("arbitrary",)
    )
    on = lambda t: t
    back = lambda t: spans - 1 - t

    def tile(at, width):
        return pl.BlockSpec((span, width), lambda t: (at(t), 0))

    def block(at, rows, width):
        return pl.BlockSpec((1, rows, width), lambda t: (at(t), 0, 0))

    def fixed(rows):
        return pl.BlockSpec((rows, channels), lambda t: (0, 0))

    def like(shape, dtype):
        return jax.ShapeDtypeStruct(shape, dtype)

    def cost(products, moved):
        return pl.CostEstimate(
            flops=2 * products * tokens * channels, bytes_accessed=moved, transcendentals=0
        )

    size = tokens * channels
    wide_tokens = like((tokens, channels), BF16)
    length = lax.axis_size("seq")
    rounds = (length - 1).bit_length()
    chunks, parts = channels // WIDTH, 2
    rows = tokens // parts
    folding = chunks * parts

    def part_of(t):
        return jnp.minimum(t, folding - 1) % parts

    def chunk_of(t):
        return jnp.minimum(t, folding - 1) // parts

    def piece(height):
        return pl.BlockSpec((height, WIDTH), lambda t: (part_of(t), chunk_of(t)))

    def column(height):
        return pl.BlockSpec((height, WIDTH), lambda t: (0, chunk_of(t)))

    def whole(*shape):
        return pl.BlockSpec(shape, lambda t: (0,) * len(shape))

    late = lambda t: jnp.maximum(t - folding, 0)
    summary = pl.BlockSpec(
        (spans // parts, states, WIDTH), lambda t: (part_of(t), 0, chunk_of(t))
    )
    slots = pltpu.VMEM((2, chunks, rounds, states + HALO, WIDTH), BF16)
    scaled = pltpu.VMEM((chunks, tokens, WIDTH), BF16)
    (
        act, da, dg, slope, before, fresh, inner_act, inner_b, inner_c, entering, arriving
    ) = pl.pallas_call(
        functools.partial(fold_kernel, length, rounds, "seq", span),
        grid=(folding + spans,),
        in_specs=[
            piece(rows),
            pl.BlockSpec(
                (HALO, WIDTH),
                lambda t: (jnp.maximum(part_of(t) * (rows // HALO) - 1, 0), chunk_of(t)),
            ),
            column(HALO),
            piece(rows),
            whole(tokens, states),
            whole(tokens, states),
            column(4),
            column(spans),
            whole(chunks, 1, WIDTH),
        ],
        out_specs=[piece(rows)] * 4
        + [summary] * 2
        + [tile(late, channels)]
        + [tile(late, states)] * 2
        + [whole(chunks, states, WIDTH)] * 2,
        out_shape=[wide_tokens] * 4
        + [like((spans, states, channels), F32)] * 2
        + [wide_tokens]
        + [like((tokens, states), F32)] * 2
        + [like((chunks, states, WIDTH), F32)] * 2,
        scratch_shapes=[
            pltpu.VMEM((rows + HALO, WIDTH), F32),
            scaled,
            scaled,
            pltpu.VMEM((8, WIDTH), F32),
            pltpu.VMEM((2, chunks, states, WIDTH), F32),
            pltpu.VMEM((2, chunks, 8, WIDTH), F32),
            slots,
            slots,
            pltpu.SemaphoreType.DMA((2, chunks, rounds)),
            pltpu.SemaphoreType.DMA((2, chunks, rounds)),
        ],
        compiler_params=pltpu.CompilerParams(
            vmem_limit_bytes=56 << 20,
            dimension_semantics=("arbitrary",),
            collective_id=0,
            has_side_effects=True,
        ),
        cost_estimate=cost(2 * span + 5 * states, 20 * size),
        name="fold",
    )(
        conv_input, conv_input, halo, grad_output, inject, readout, weights, wide,
        own_log.reshape(chunks, 1, WIDTH),
    )
    pairs, both = pl.pallas_call(
        shared_kernel,
        grid=(spans,),
        in_specs=[tile(back, channels)] * 4
        + [block(back, 1, channels)] * 2
        + [block(back, states, channels)] * 2
        + [whole(chunks, states, WIDTH)] * 2
        + [tile(back, states)] * 2,
        out_specs=[block(back, 2 * states, channels), tile(back, 2 * states)],
        out_shape=[
            like((spans, 2 * states, channels), BF16),
            like((tokens, 2 * states), F32),
        ],
        scratch_shapes=[
            pltpu.VMEM((2 * states, channels), BF16),
            pltpu.VMEM((states, channels), F32),
        ],
        compiler_params=params,
        cost_estimate=cost(8 * states, 14 * size),
        name="shared",
    )(grad_output, dg, act, da, lr, prior, before, fresh, entering, arriving, inner_b, inner_c)

    mine, pairs = lax.optimization_barrier((half_sums(both), pairs))
    grad_input, first = pl.pallas_call(
        input_kernel,
        grid=(spans,),
        in_specs=[
            tile(back, states),
            fixed(4),
            block(back, 1, channels),
            block(back, 2 * states, channels),
            tile(back, channels),
            tile(back, channels),
        ],
        out_specs=[tile(back, channels), fixed(8)],
        out_shape=[like((tokens, channels), F32), like((8, channels), F32)],
        scratch_shapes=[pltpu.VMEM((span + 8, channels), F32)],
        compiler_params=params,
        cost_estimate=cost(2 * states, 10 * size),
        name="inputs",
    )(inject, weights, lr, pairs, inner_act, slope)
    mine, first = lax.optimization_barrier((pair_sums(mine), first))
    later = shifted(first, "seq", -1)
    edge = jnp.stack(
        [sum(weights[k] * later[r - k] for k in range(r + 1)) for r in range(3)], axis=0
    )
    last = grad_input[tokens - 8 :] + jnp.pad(edge, ((5, 0), (0, 0)))
    grad_input = lax.dynamic_update_slice(grad_input, last, (tokens - 8, 0))
    total = joined_halves(mine)
    return grad_input, total[:, :states], total[:, states:]


def solution(mesh):
    return jax.shard_map(
        body,
        mesh=mesh,
        in_specs=(
            P("seq", "hg"),
            P("seq", "hg"),
            P("seq", None),
            P("seq", None),
            P(None, "hg"),
            P("hg", "seq"),
        ),
        out_specs=(P("seq", "hg"), P("seq", None), P("seq", None)),
        check_vma=False,
    )
```

```python
import functools

import jax
import jax.numpy as jnp
from jax import lax
from jax.experimental import pallas as pl
from jax.experimental.pallas import tpu as pltpu
from jax.sharding import PartitionSpec as P

F32 = jnp.float32
BF16 = jnp.bfloat16
HALO = 16


def mm(a, b, ca, cb):
    return lax.dot_general(a, b, (((ca,), (cb,)), ((), ())), preferred_element_type=F32)


WIDTH = 256


def chunks_of(channels):
    return [slice(i, i + WIDTH) for i in range(0, channels, WIDTH)]


def preact_of(xs, w_ref, at, span):
    v = w_ref[0:1] * xs[at + HALO - 3 : at + HALO - 3 + span]
    for k in range(1, 4):
        v = v + w_ref[k : k + 1] * xs[at + HALO - 3 + k : at + HALO - 3 + k + span]
    return v


def decays(lr, span):
    width = lr.shape[1]
    rows = lax.broadcasted_iota(jnp.int32, (8, width), 0)
    held = jnp.exp((rows - span // 2).astype(F32) * lr)
    length = 8
    while length < span:
        held = jnp.concatenate([held, held * jnp.exp(length * lr)], axis=0)
        length *= 2
    return held


def log_rows(log):
    high = log.astype(BF16).astype(F32)
    mid = (log - high).astype(BF16).astype(F32)
    low = log - high - mid
    rows = lax.broadcasted_iota(jnp.int32, (HALO, log.shape[1]), 0)
    tile = jnp.where(rows == 0, high, jnp.where(rows == 1, mid, jnp.where(rows == 2, low, 0.0)))
    return tile.astype(BF16)


def fold_kernel(
    length, rounds, axis, span,
    x_ref, prev_ref, all_ref, g_ref, b_ref, c_ref, w_ref, lr_ref, log_ref,
    act_ref, da_ref, dg_ref, slope_ref, before_ref, fresh_ref,
    ga_ref, gb_ref, gc_ref, entering_ref, arriving_ref,
    xs, gs, ab, running, held, logs, sent, landed, halo, send_sem, recv_sem, halo_sem,
):
    t = pl.program_id(0)
    chunks, size = held.shape[1], held.shape[2]
    rows, width = x_ref.shape
    parts = b_ref.shape[0] // rows
    spans = b_ref.shape[0] // span
    folding = chunks * parts
    half = span // 2
    me = lax.axis_index(axis)
    founds = (entering_ref, arriving_ref)

    def inside(device):
        return jnp.logical_and(device >= 0, device < length)

    def copy(way, n, r):
        by = (1 << r) * (1 - 2 * way)
        move = pltpu.make_async_remote_copy(
            src_ref=sent.at[way, n, r],
            dst_ref=landed.at[way, n, r],
            send_sem=send_sem.at[way, n, r],
            recv_sem=recv_sem.at[way, n, r],
            device_id={axis: me + by},
            device_id_type=pl.DeviceIdType.MESH,
        )
        return move, inside(me + by), inside(me - by)

    def start(n, r):
        for way in range(2):
            sent[way, n, r, 0:size] = held[way, n].astype(BF16)
            sent[way, n, r, size : size + HALO] = log_rows(logs[way, n, 0:1])
            move, sends, _ = copy(way, n, r)

            @pl.when(sends)
            def _():
                move.start()

    def finish(n, r):
        for way in range(2):
            move, sends, takes = copy(way, n, r)

            @pl.when(takes)
            def _():
                move.wait_recv()
                got = landed[way, n, r, 0:size].astype(F32)
                tail = landed[way, n, r, size : size + HALO].astype(F32)
                got_log = (tail[0:1] + tail[1:2]) + tail[2:3]
                found = founds[way]
                found[n] = found[n] + jnp.exp(logs[way, n, 1:2]) * got
                if r < rounds - 1:
                    held[way, n] = held[way, n] + jnp.exp(logs[way, n, 0:1]) * got
                    logs[way, n, 0:1] = logs[way, n, 0:1] + got_log
                    logs[way, n, 1:2] = logs[way, n, 1:2] + got_log

            @pl.when(sends)
            def _():
                move.wait_send()

    @pl.when(t == 0)
    def _():
        barrier = pltpu.get_barrier_semaphore()
        others = [me + sign * (1 << r) for r in range(rounds) for sign in (1, -1)]
        for other in others:

            @pl.when(inside(other))
            def _():
                pl.semaphore_signal(
                    barrier, inc=1, device_id={axis: other}, device_id_type=pl.DeviceIdType.MESH
                )

        pl.semaphore_wait(barrier, sum(jnp.where(inside(other), 1, 0) for other in others))
        move = pltpu.make_async_remote_copy(
            src_ref=all_ref.at[pl.ds(all_ref.shape[0] - HALO, HALO)],
            dst_ref=halo,
            send_sem=halo_sem.at[0],
            recv_sem=halo_sem.at[1],
            device_id={axis: me + 1},
            device_id_type=pl.DeviceIdType.MESH,
        )

        @pl.when(inside(me + 1))
        def _():
            move.start()

        held[...] = jnp.zeros_like(held)
        for way, found in enumerate(founds):
            found[...] = jnp.zeros_like(found)
            for n in range(chunks):
                logs[way, n, 0:1] = log_ref[n]
                logs[way, n, 1:2] = jnp.zeros((1, width), F32)

        @pl.when(me == 0)
        def _():
            halo[...] = jnp.zeros_like(halo)

        @pl.when(me > 0)
        def _():
            move.wait_recv()

        @pl.when(inside(me + 1))
        def _():
            move.wait_send()

    @pl.when(t < folding)
    def _():
        n, part = t // parts, t % parts

        @pl.when(part == 0)
        def _():
            xs[0:HALO] = halo[:, pl.ds(pl.multiple_of(n * width, width), width)].astype(F32)
            running[...] = jnp.zeros_like(running)

        @pl.when(part > 0)
        def _():
            xs[0:HALO] = prev_ref[...].astype(F32)

        xs[HALO : HALO + rows] = x_ref[...].astype(F32)
        for q in range(rows // span):
            at = q * span
            here = slice(at, at + span)
            place = pl.multiple_of(part * rows + at, span)
            lr = lr_ref[pl.ds(part * (rows // span) + q, 1)]
            b = b_ref[pl.ds(place, span)].T
            c = c_ref[pl.ds(place, span)].T
            v = preact_of(xs, w_ref, at, span)
            squashed = 0.5 + 0.5 * jnp.tanh(0.5 * v)
            full = v * squashed
            slope_ref[here] = (squashed + full * (1.0 - squashed) - 0.5).astype(BF16)
            a = full.astype(BF16)
            act_ref[here] = a
            af = a.astype(F32)
            more = af * (decays(-lr, span) - 1.0)
            da = more.astype(BF16)
            da_ref[here] = da
            ab[n, pl.ds(place, span)] = (af + more).astype(BF16)
            g = g_ref[here]
            gf = g.astype(F32)
            more = gf * (decays(lr, span) - 1.0)
            dg = more.astype(BF16)
            dg_ref[here] = dg
            gs[n, pl.ds(place, span)] = (gf + more).astype(BF16)
            fresh_state = jnp.exp((half - 1.0) * lr) * (mm(b, a, 1, 0) + mm(b, da, 1, 0))
            fresh_grad = jnp.exp((half + 1.0) * lr) * (mm(c, g, 1, 0) + mm(c, dg, 1, 0))
            state = held[0, n]
            before_ref[q] = state
            fresh_ref[q] = fresh_grad
            held[0, n] = jnp.exp(span * lr) * state + fresh_state
            held[1, n] = held[1, n] + jnp.exp(running[0:1]) * fresh_grad
            running[...] = running[...] + span * lr

    @pl.when(t >= folding)
    def _():
        place = pl.multiple_of((t - folding) * span, span)
        b, c = b_ref[pl.ds(place, span)], c_ref[pl.ds(place, span)]
        down = lax.broadcasted_iota(jnp.int32, (span, span), 0)
        along = lax.broadcasted_iota(jnp.int32, (span, span), 1)
        mixed = jnp.where(down <= along, mm(b, c, 1, 1), 0.0).astype(BF16)
        pairs = jnp.zeros((span, span), F32)
        for n in range(chunks):
            scaled = gs[n, pl.ds(place, span)]
            pairs = pairs + mm(scaled, ab[n, pl.ds(place, span)], 1, 1)
            ga_ref[:, n * width : (n + 1) * width] = mm(mixed, scaled, 1, 0).astype(BF16)
        pairs = jnp.where(down >= along, pairs, 0.0).astype(BF16)
        gb_ref[...] = mm(pairs, c, 0, 0)
        gc_ref[...] = mm(pairs, b, 1, 0)

    def step_of(n, r):
        step = parts * (n + 1) - 1 + 2 * r
        over = step - (folding - 1)
        return step if over <= 0 else folding - 1 + over * spans // (2 * rounds)

    for n in range(chunks):
        for r in range(rounds + 1):

            @pl.when(t == step_of(n, r))
            def _():
                if r > 0:
                    finish(n, r - 1)
                if r < rounds:
                    start(n, r)


def quadrants(high_ref, low_ref, pair):
    span, size = high_ref.shape[0], pair.shape[0] // 2
    stacked = jnp.concatenate([high_ref[...], low_ref[...]], axis=0)
    products = mm(stacked, pair, 1, 1)
    rows = products[:span] + products[span:]
    return rows[:, :size] + rows[:, size:]


def shared_kernel(
    g_ref, dg_ref, act_ref, da_ref, lr_ref, prior_ref, before_ref, fresh_ref,
    entering_ref, arriving_ref, inner_b_ref, inner_c_ref,
    pair_ref, both_ref, states, carry,
):
    t = pl.program_id(0)
    span, channels = g_ref.shape
    half = span // 2
    size = carry.shape[0]

    @pl.when(t == 0)
    def _():
        for n, cols in enumerate(chunks_of(channels)):
            carry[:, cols] = arriving_ref[n]

    for n, cols in enumerate(chunks_of(channels)):
        lr = lr_ref[0, 0:1, cols]
        sb = jnp.exp((half + 1.0) * lr) * (
            before_ref[0, :, cols] + prior_ref[0, 0:1, cols] * entering_ref[n]
        )
        hi = sb.astype(BF16)
        states[0:size, cols] = hi
        states[size : 2 * size, cols] = (sb - hi.astype(F32)).astype(BF16)
        held = carry[:, cols]
        ga = jnp.exp((half - 1.0) * lr) * held
        hi = ga.astype(BF16)
        pair_ref[0, 0:size, cols] = hi
        pair_ref[0, size : 2 * size, cols] = (ga - hi.astype(F32)).astype(BF16)
        carry[:, cols] = jnp.exp(span * lr) * held + fresh_ref[0, :, cols]
    both_ref[:, 0:size] = inner_b_ref[...] + quadrants(act_ref, da_ref, pair_ref[0])
    both_ref[:, size:] = inner_c_ref[...] + quadrants(g_ref, dg_ref, states[...])


def input_kernel(
    b_ref, w_ref, lr_ref, pair_ref, ga_ref, slope_ref,
    gx_ref, first_ref, gp,
):
    t = pl.program_id(0)
    span, channels = ga_ref.shape

    @pl.when(t == 0)
    def _():
        gp[span : span + 8] = jnp.zeros((8, channels), F32)

    @pl.when(t > 0)
    def _():
        gp[span : span + 8] = gp[0:8]

    twice = jnp.concatenate([b_ref[...], b_ref[...]], axis=1)
    for cols in chunks_of(channels):
        grad_act = mm(twice, pair_ref[0, :, cols], 1, 0) + ga_ref[:, cols].astype(F32)
        slope = slope_ref[:, cols].astype(F32) + 0.5
        gp[0:span, cols] = grad_act * decays(-lr_ref[0, 0:1, cols], span) * slope
        out = w_ref[0:1, cols] * gp[3 : 3 + span, cols]
        for k in range(1, 4):
            out = out + w_ref[k : k + 1, cols] * gp[3 - k : 3 - k + span, cols]
        gx_ref[:, cols] = out
    first_ref[...] = gp[0:8]


def shifted(array, axis, by):
    length = lax.axis_size(axis)
    return lax.ppermute(
        array, axis, [(i, i + by) for i in range(length) if 0 <= i + by < length]
    )


def swapped(array, axis, flip):
    return lax.ppermute(array, axis, [(i, i ^ flip) for i in range(lax.axis_size(axis))])


def half_sums(both):
    rows = both.shape[0] // 2
    odd = (lax.axis_index("hg") % 2) == 1
    low, high = both[:rows], both[rows:]
    return jnp.where(odd, high, low) + swapped(jnp.where(odd, low, high), "hg", 1)


def pair_sums(mine):
    flip = 2
    while flip < lax.axis_size("hg"):
        sent = mine.astype(BF16)
        mine = sent.astype(F32) + swapped(sent, "hg", flip).astype(F32)
        flip *= 2
    return mine


def joined_halves(mine):
    odd = (lax.axis_index("hg") % 2) == 1
    other = swapped(mine, "hg", 1)
    return jnp.concatenate([jnp.where(odd, other, mine), jnp.where(odd, mine, other)], axis=0)


def body(conv_input, grad_output, inject, readout, conv_weight, decay_codes):
    tokens, channels = conv_input.shape
    heads, spans = decay_codes.shape
    span = tokens // spans
    head_dim = channels // heads
    states = inject.shape[1]
    weights = conv_weight.astype(F32)
    log_rates = jnp.log1p(-decay_codes.astype(F32) * 1e-06)
    wide = jnp.repeat(log_rates.T, head_dim, axis=1)
    prior = jnp.exp(span * (jnp.cumsum(wide, axis=0) - wide))[:, None]
    own_log = span * jnp.sum(wide, axis=0, keepdims=True)
    lr = wide[:, None]
    params = pltpu.CompilerParams(
        vmem_limit_bytes=60 << 20, dimension_semantics=("arbitrary",)
    )
    on = lambda t: t
    back = lambda t: spans - 1 - t

    def tile(at, width):
        return pl.BlockSpec((span, width), lambda t: (at(t), 0))

    def block(at, rows, width):
        return pl.BlockSpec((1, rows, width), lambda t: (at(t), 0, 0))

    def fixed(rows):
        return pl.BlockSpec((rows, channels), lambda t: (0, 0))

    def like(shape, dtype):
        return jax.ShapeDtypeStruct(shape, dtype)

    def cost(products, moved):
        return pl.CostEstimate(
            flops=2 * products * tokens * channels, bytes_accessed=moved, transcendentals=0
        )

    size = tokens * channels
    wide_tokens = like((tokens, channels), BF16)
    length = lax.axis_size("seq")
    rounds = (length - 1).bit_length()
    chunks, parts = channels // WIDTH, 2
    rows = tokens // parts
    folding = chunks * parts

    def part_of(t):
        return jnp.minimum(t, folding - 1) % parts

    def chunk_of(t):
        return jnp.minimum(t, folding - 1) // parts

    def piece(height):
        return pl.BlockSpec((height, WIDTH), lambda t: (part_of(t), chunk_of(t)))

    def column(height):
        return pl.BlockSpec((height, WIDTH), lambda t: (0, chunk_of(t)))

    def whole(*shape):
        return pl.BlockSpec(shape, lambda t: (0,) * len(shape))

    late = lambda t: jnp.maximum(t - folding, 0)
    summary = pl.BlockSpec(
        (spans // parts, states, WIDTH), lambda t: (part_of(t), 0, chunk_of(t))
    )
    slots = pltpu.VMEM((2, chunks, rounds, states + HALO, WIDTH), BF16)
    scaled = pltpu.VMEM((chunks, tokens, WIDTH), BF16)
    (
        act, da, dg, slope, before, fresh, inner_act, inner_b, inner_c, entering, arriving
    ) = pl.pallas_call(
        functools.partial(fold_kernel, length, rounds, "seq", span),
        grid=(folding + spans,),
        in_specs=[
            piece(rows),
            pl.BlockSpec(
                (HALO, WIDTH),
                lambda t: (jnp.maximum(part_of(t) * (rows // HALO) - 1, 0), chunk_of(t)),
            ),
            pl.BlockSpec(memory_space=pl.ANY),
            piece(rows),
            whole(tokens, states),
            whole(tokens, states),
            column(4),
            column(spans),
            whole(chunks, 1, WIDTH),
        ],
        out_specs=[piece(rows)] * 4
        + [summary] * 2
        + [tile(late, channels)]
        + [tile(late, states)] * 2
        + [whole(chunks, states, WIDTH)] * 2,
        out_shape=[wide_tokens] * 4
        + [like((spans, states, channels), F32)] * 2
        + [wide_tokens]
        + [like((tokens, states), F32)] * 2
        + [like((chunks, states, WIDTH), F32)] * 2,
        scratch_shapes=[
            pltpu.VMEM((rows + HALO, WIDTH), F32),
            scaled,
            scaled,
            pltpu.VMEM((8, WIDTH), F32),
            pltpu.VMEM((2, chunks, states, WIDTH), F32),
            pltpu.VMEM((2, chunks, 8, WIDTH), F32),
            slots,
            slots,
            pltpu.VMEM((HALO, channels), BF16),
            pltpu.SemaphoreType.DMA((2, chunks, rounds)),
            pltpu.SemaphoreType.DMA((2, chunks, rounds)),
            pltpu.SemaphoreType.DMA((2,)),
        ],
        compiler_params=pltpu.CompilerParams(
            vmem_limit_bytes=60 << 20,
            dimension_semantics=("arbitrary",),
            collective_id=0,
            has_side_effects=True,
        ),
        cost_estimate=cost(2 * span + 5 * states, 20 * size),
        name="fold",
    )(
        conv_input, conv_input, conv_input, grad_output, inject, readout, weights, wide,
        own_log.reshape(chunks, 1, WIDTH),
    )
    pairs, both = pl.pallas_call(
        shared_kernel,
        grid=(spans,),
        in_specs=[tile(back, channels)] * 4
        + [block(back, 1, channels)] * 2
        + [block(back, states, channels)] * 2
        + [whole(chunks, states, WIDTH)] * 2
        + [tile(back, states)] * 2,
        out_specs=[block(back, 2 * states, channels), tile(back, 2 * states)],
        out_shape=[
            like((spans, 2 * states, channels), BF16),
            like((tokens, 2 * states), F32),
        ],
        scratch_shapes=[
            pltpu.VMEM((2 * states, channels), BF16),
            pltpu.VMEM((states, channels), F32),
        ],
        compiler_params=params,
        cost_estimate=cost(8 * states, 14 * size),
        name="shared",
    )(grad_output, dg, act, da, lr, prior, before, fresh, entering, arriving, inner_b, inner_c)

    mine, pairs = lax.optimization_barrier((half_sums(both), pairs))
    grad_input, first = pl.pallas_call(
        input_kernel,
        grid=(spans,),
        in_specs=[
            tile(back, states),
            fixed(4),
            block(back, 1, channels),
            block(back, 2 * states, channels),
            tile(back, channels),
            tile(back, channels),
        ],
        out_specs=[tile(back, channels), fixed(8)],
        out_shape=[like((tokens, channels), F32), like((8, channels), F32)],
        scratch_shapes=[pltpu.VMEM((span + 8, channels), F32)],
        compiler_params=params,
        cost_estimate=cost(2 * states, 10 * size),
        name="inputs",
    )(inject, weights, lr, pairs, inner_act, slope)
    mine, first = lax.optimization_barrier((pair_sums(mine), first))
    later = shifted(first, "seq", -1)
    edge = jnp.stack(
        [sum(weights[k] * later[r - k] for k in range(r + 1)) for r in range(3)], axis=0
    )
    last = grad_input[tokens - 8 :] + jnp.pad(edge, ((5, 0), (0, 0)))
    grad_input = lax.dynamic_update_slice(grad_input, last, (tokens - 8, 0))
    total = joined_halves(mine)
    return grad_input, total[:, :states], total[:, states:]


def solution(mesh):
    return jax.shard_map(
        body,
        mesh=mesh,
        in_specs=(
            P("seq", "hg"),
            P("seq", "hg"),
            P("seq", None),
            P("seq", None),
            P(None, "hg"),
            P("hg", "seq"),
        ),
        out_specs=(P("seq", "hg"), P("seq", None), P("seq", None)),
        check_vma=False,
    )
```

```python
import functools

import jax
import jax.numpy as jnp
from jax import lax
from jax.experimental import pallas as pl
from jax.experimental.pallas import tpu as pltpu
from jax.sharding import PartitionSpec as P

F32 = jnp.float32
BF16 = jnp.bfloat16
HALO = 16


def mm(a, b, ca, cb):
    return lax.dot_general(a, b, (((ca,), (cb,)), ((), ())), preferred_element_type=F32)


WIDTH = 256


def chunks_of(channels):
    return [slice(i, i + WIDTH) for i in range(0, channels, WIDTH)]


def preact_of(xs, w_ref, at, span):
    v = w_ref[0:1] * xs[at + HALO - 3 : at + HALO - 3 + span]
    for k in range(1, 4):
        v = v + w_ref[k : k + 1] * xs[at + HALO - 3 + k : at + HALO - 3 + k + span]
    return v


PIECE = 32


def decays(lr, span, middle):
    width = lr.shape[1]
    rows = lax.broadcasted_iota(jnp.int32, (8, width), 0)
    held = jnp.exp((rows - middle).astype(F32) * lr)
    length = 8
    while length < span:
        held = jnp.concatenate([held, held * jnp.exp(length * lr)], axis=0)
        length *= 2
    return held


def log_rows(log):
    high = log.astype(BF16).astype(F32)
    mid = (log - high).astype(BF16).astype(F32)
    low = log - high - mid
    rows = lax.broadcasted_iota(jnp.int32, (HALO, log.shape[1]), 0)
    tile = jnp.where(rows == 0, high, jnp.where(rows == 1, mid, jnp.where(rows == 2, low, 0.0)))
    return tile.astype(BF16)


def fold_kernel(
    length, rounds, axis, span,
    x_ref, prev_ref, all_ref, g_ref, b_ref, c_ref, w_ref, lr_ref, log_ref,
    act_ref, da_ref, dg_ref, slope_ref, before_ref, fresh_ref,
    ga_ref, gb_ref, gc_ref, entering_ref, arriving_ref,
    xs, gs, ab, running, held, logs, sent, landed, halo, send_sem, recv_sem, halo_sem,
):
    t = pl.program_id(0)
    chunks, size = held.shape[1], held.shape[2]
    rows, width = x_ref.shape
    parts = b_ref.shape[0] // rows
    spans = b_ref.shape[0] // span
    folding = chunks * parts
    half = span // 2
    me = lax.axis_index(axis)
    founds = (entering_ref, arriving_ref)

    def inside(device):
        return jnp.logical_and(device >= 0, device < length)

    def copy(way, n, r):
        by = (1 << r) * (1 - 2 * way)
        move = pltpu.make_async_remote_copy(
            src_ref=sent.at[way, n, r],
            dst_ref=landed.at[way, n, r],
            send_sem=send_sem.at[way, n, r],
            recv_sem=recv_sem.at[way, n, r],
            device_id={axis: me + by},
            device_id_type=pl.DeviceIdType.MESH,
        )
        return move, inside(me + by), inside(me - by)

    def start(n, r):
        for way in range(2):
            sent[way, n, r, 0:size] = held[way, n].astype(BF16)
            sent[way, n, r, size : size + HALO] = log_rows(logs[way, n, 0:1])
            move, sends, _ = copy(way, n, r)

            @pl.when(sends)
            def _():
                move.start()

    def finish(n, r):
        for way in range(2):
            move, sends, takes = copy(way, n, r)

            @pl.when(takes)
            def _():
                move.wait_recv()
                got = landed[way, n, r, 0:size].astype(F32)
                tail = landed[way, n, r, size : size + HALO].astype(F32)
                got_log = (tail[0:1] + tail[1:2]) + tail[2:3]
                found = founds[way]
                found[n] = found[n] + jnp.exp(logs[way, n, 1:2]) * got
                if r < rounds - 1:
                    held[way, n] = held[way, n] + jnp.exp(logs[way, n, 0:1]) * got
                    logs[way, n, 0:1] = logs[way, n, 0:1] + got_log
                    logs[way, n, 1:2] = logs[way, n, 1:2] + got_log

            @pl.when(sends)
            def _():
                move.wait_send()

    @pl.when(t == 0)
    def _():
        barrier = pltpu.get_barrier_semaphore()
        others = [me + sign * (1 << r) for r in range(rounds) for sign in (1, -1)]
        for other in others:

            @pl.when(inside(other))
            def _():
                pl.semaphore_signal(
                    barrier, inc=1, device_id={axis: other}, device_id_type=pl.DeviceIdType.MESH
                )

        pl.semaphore_wait(barrier, sum(jnp.where(inside(other), 1, 0) for other in others))
        move = pltpu.make_async_remote_copy(
            src_ref=all_ref.at[pl.ds(all_ref.shape[0] - HALO, HALO)],
            dst_ref=halo,
            send_sem=halo_sem.at[0],
            recv_sem=halo_sem.at[1],
            device_id={axis: me + 1},
            device_id_type=pl.DeviceIdType.MESH,
        )

        @pl.when(inside(me + 1))
        def _():
            move.start()

        held[...] = jnp.zeros_like(held)
        for way, found in enumerate(founds):
            found[...] = jnp.zeros_like(found)
            for n in range(chunks):
                logs[way, n, 0:1] = log_ref[n]
                logs[way, n, 1:2] = jnp.zeros((1, width), F32)

        @pl.when(me == 0)
        def _():
            halo[...] = jnp.zeros_like(halo)

        @pl.when(me > 0)
        def _():
            move.wait_recv()

        @pl.when(inside(me + 1))
        def _():
            move.wait_send()

    @pl.when(t < folding)
    def _():
        n, part = t // parts, t % parts

        @pl.when(part == 0)
        def _():
            xs[0:HALO] = halo[:, pl.ds(pl.multiple_of(n * width, width), width)].astype(F32)
            running[...] = jnp.zeros_like(running)

        @pl.when(part > 0)
        def _():
            xs[0:HALO] = prev_ref[...].astype(F32)

        xs[HALO : HALO + rows] = x_ref[...].astype(F32)
        for q in range(rows // span):
            at = q * span
            place = pl.multiple_of(part * rows + at, span)
            lr = lr_ref[pl.ds(part * (rows // span) + q, 1)]
            b = b_ref[pl.ds(place, span)].T
            c = c_ref[pl.ds(place, span)].T
            up, down_by = decays(lr, PIECE, half), decays(-lr, PIECE, half)
            for first in range(0, span, PIECE):
                here = slice(at + first, at + first + PIECE)
                there = pl.ds(place + first, PIECE)
                v = preact_of(xs, w_ref, at + first, PIECE)
                squashed = 0.5 + 0.5 * jnp.tanh(0.5 * v)
                full = v * squashed
                slope_ref[here] = (squashed + full * (1.0 - squashed) - 0.5).astype(BF16)
                a = full.astype(BF16)
                act_ref[here] = a
                af = a.astype(F32)
                more = af * (down_by * jnp.exp(-first * lr) - 1.0)
                da_ref[here] = more.astype(BF16)
                ab[n, there] = (af + more).astype(BF16)
                gf = g_ref[here].astype(F32)
                more = gf * (up * jnp.exp(first * lr) - 1.0)
                dg_ref[here] = more.astype(BF16)
                gs[n, there] = (gf + more).astype(BF16)
            here = slice(at, at + span)
            a, da, g, dg = act_ref[here], da_ref[here], g_ref[here], dg_ref[here]
            fresh_state = jnp.exp((half - 1.0) * lr) * (mm(b, a, 1, 0) + mm(b, da, 1, 0))
            fresh_grad = jnp.exp((half + 1.0) * lr) * (mm(c, g, 1, 0) + mm(c, dg, 1, 0))
            state = held[0, n]
            before_ref[q] = state
            fresh_ref[q] = fresh_grad
            held[0, n] = jnp.exp(span * lr) * state + fresh_state
            held[1, n] = held[1, n] + jnp.exp(running[0:1]) * fresh_grad
            running[...] = running[...] + span * lr

    @pl.when(t >= folding)
    def _():
        place = pl.multiple_of((t - folding) * span, span)
        b, c = b_ref[pl.ds(place, span)], c_ref[pl.ds(place, span)]
        down = lax.broadcasted_iota(jnp.int32, (span, span), 0)
        along = lax.broadcasted_iota(jnp.int32, (span, span), 1)
        mixed = jnp.where(down <= along, mm(b, c, 1, 1), 0.0).astype(BF16)
        pairs = jnp.zeros((span, span), F32)
        for n in range(chunks):
            scaled = gs[n, pl.ds(place, span)]
            pairs = pairs + mm(scaled, ab[n, pl.ds(place, span)], 1, 1)
            ga_ref[:, n * width : (n + 1) * width] = mm(mixed, scaled, 1, 0).astype(BF16)
        pairs = jnp.where(down >= along, pairs, 0.0).astype(BF16)
        gb_ref[...] = mm(pairs, c, 0, 0)
        gc_ref[...] = mm(pairs, b, 1, 0)

    def step_of(n, r):
        step = parts * (n + 1) - 1 + 2 * r
        over = step - (folding - 1)
        return step if over <= 0 else folding - 1 + over * spans // (2 * rounds)

    for n in range(chunks):
        for r in range(rounds + 1):

            @pl.when(t == step_of(n, r))
            def _():
                if r > 0:
                    finish(n, r - 1)
                if r < rounds:
                    start(n, r)


def quadrants(high_ref, low_ref, pair):
    span, size = high_ref.shape[0], pair.shape[0] // 2
    stacked = jnp.concatenate([high_ref[...], low_ref[...]], axis=0)
    products = mm(stacked, pair, 1, 1)
    rows = products[:span] + products[span:]
    return rows[:, :size] + rows[:, size:]


def shared_kernel(
    g_ref, dg_ref, act_ref, da_ref, lr_ref, prior_ref, before_ref, fresh_ref,
    entering_ref, arriving_ref, inner_b_ref, inner_c_ref,
    pair_ref, both_ref, states, carry,
):
    t = pl.program_id(0)
    span, channels = g_ref.shape
    half = span // 2
    size = carry.shape[0]

    @pl.when(t == 0)
    def _():
        for n, cols in enumerate(chunks_of(channels)):
            carry[:, cols] = arriving_ref[n]

    for n, cols in enumerate(chunks_of(channels)):
        lr = lr_ref[0, 0:1, cols]
        sb = jnp.exp((half + 1.0) * lr) * (
            before_ref[0, :, cols] + prior_ref[0, 0:1, cols] * entering_ref[n]
        )
        hi = sb.astype(BF16)
        states[0:size, cols] = hi
        states[size : 2 * size, cols] = (sb - hi.astype(F32)).astype(BF16)
        held = carry[:, cols]
        ga = jnp.exp((half - 1.0) * lr) * held
        hi = ga.astype(BF16)
        pair_ref[0, 0:size, cols] = hi
        pair_ref[0, size : 2 * size, cols] = (ga - hi.astype(F32)).astype(BF16)
        carry[:, cols] = jnp.exp(span * lr) * held + fresh_ref[0, :, cols]
    both_ref[:, 0:size] = inner_b_ref[...] + quadrants(act_ref, da_ref, pair_ref[0])
    both_ref[:, size:] = inner_c_ref[...] + quadrants(g_ref, dg_ref, states[...])


def input_kernel(
    b_ref, w_ref, lr_ref, pair_ref, ga_ref, slope_ref,
    gx_ref, first_ref, gp,
):
    t = pl.program_id(0)
    span, channels = ga_ref.shape

    @pl.when(t == 0)
    def _():
        gp[span : span + 8] = jnp.zeros((8, channels), F32)

    @pl.when(t > 0)
    def _():
        gp[span : span + 8] = gp[0:8]

    twice = jnp.concatenate([b_ref[...], b_ref[...]], axis=1)
    for cols in chunks_of(channels):
        grad_act = mm(twice, pair_ref[0, :, cols], 1, 0) + ga_ref[:, cols].astype(F32)
        slope = slope_ref[:, cols].astype(F32) + 0.5
        gp[0:span, cols] = grad_act * decays(-lr_ref[0, 0:1, cols], span, span // 2) * slope
        out = w_ref[0:1, cols] * gp[3 : 3 + span, cols]
        for k in range(1, 4):
            out = out + w_ref[k : k + 1, cols] * gp[3 - k : 3 - k + span, cols]
        gx_ref[:, cols] = out
    first_ref[...] = gp[0:8]


def shifted(array, axis, by):
    length = lax.axis_size(axis)
    return lax.ppermute(
        array, axis, [(i, i + by) for i in range(length) if 0 <= i + by < length]
    )


def swapped(array, axis, flip):
    return lax.ppermute(array, axis, [(i, i ^ flip) for i in range(lax.axis_size(axis))])


def half_sums(both):
    rows = both.shape[0] // 2
    odd = (lax.axis_index("hg") % 2) == 1
    low, high = both[:rows], both[rows:]
    return jnp.where(odd, high, low) + swapped(jnp.where(odd, low, high), "hg", 1)


def pair_sums(mine):
    flip = 2
    while flip < lax.axis_size("hg"):
        sent = mine.astype(BF16)
        mine = sent.astype(F32) + swapped(sent, "hg", flip).astype(F32)
        flip *= 2
    return mine


def joined_halves(mine):
    odd = (lax.axis_index("hg") % 2) == 1
    other = swapped(mine, "hg", 1)
    return jnp.concatenate([jnp.where(odd, other, mine), jnp.where(odd, mine, other)], axis=0)


def body(conv_input, grad_output, inject, readout, conv_weight, decay_codes):
    tokens, channels = conv_input.shape
    heads, spans = decay_codes.shape
    span = tokens // spans
    head_dim = channels // heads
    states = inject.shape[1]
    weights = conv_weight.astype(F32)
    log_rates = jnp.log1p(-decay_codes.astype(F32) * 1e-06)
    wide = jnp.repeat(log_rates.T, head_dim, axis=1)
    prior = jnp.exp(span * (jnp.cumsum(wide, axis=0) - wide))[:, None]
    own_log = span * jnp.sum(wide, axis=0, keepdims=True)
    lr = wide[:, None]
    params = pltpu.CompilerParams(
        vmem_limit_bytes=48 << 20, dimension_semantics=("arbitrary",)
    )
    on = lambda t: t
    back = lambda t: spans - 1 - t

    def tile(at, width):
        return pl.BlockSpec((span, width), lambda t: (at(t), 0))

    def block(at, rows, width):
        return pl.BlockSpec((1, rows, width), lambda t: (at(t), 0, 0))

    def fixed(rows):
        return pl.BlockSpec((rows, channels), lambda t: (0, 0))

    def like(shape, dtype):
        return jax.ShapeDtypeStruct(shape, dtype)

    def cost(products, moved):
        return pl.CostEstimate(
            flops=2 * products * tokens * channels, bytes_accessed=moved, transcendentals=0
        )

    size = tokens * channels
    wide_tokens = like((tokens, channels), BF16)
    length = lax.axis_size("seq")
    rounds = (length - 1).bit_length()
    chunks, parts = channels // WIDTH, 2
    rows = tokens // parts
    folding = chunks * parts

    def part_of(t):
        return jnp.minimum(t, folding - 1) % parts

    def chunk_of(t):
        return jnp.minimum(t, folding - 1) // parts

    def piece(height):
        return pl.BlockSpec((height, WIDTH), lambda t: (part_of(t), chunk_of(t)))

    def column(height):
        return pl.BlockSpec((height, WIDTH), lambda t: (0, chunk_of(t)))

    def whole(*shape):
        return pl.BlockSpec(shape, lambda t: (0,) * len(shape))

    late = lambda t: jnp.maximum(t - folding, 0)
    summary = pl.BlockSpec(
        (spans // parts, states, WIDTH), lambda t: (part_of(t), 0, chunk_of(t))
    )
    slots = pltpu.VMEM((2, chunks, rounds, states + HALO, WIDTH), BF16)
    scaled = pltpu.VMEM((chunks, tokens, WIDTH), BF16)
    (
        act, da, dg, slope, before, fresh, inner_act, inner_b, inner_c, entering, arriving
    ) = pl.pallas_call(
        functools.partial(fold_kernel, length, rounds, "seq", span),
        grid=(folding + spans,),
        in_specs=[
            piece(rows),
            pl.BlockSpec(
                (HALO, WIDTH),
                lambda t: (jnp.maximum(part_of(t) * (rows // HALO) - 1, 0), chunk_of(t)),
            ),
            pl.BlockSpec(memory_space=pl.ANY),
            piece(rows),
            whole(tokens, states),
            whole(tokens, states),
            column(4),
            column(spans),
            whole(chunks, 1, WIDTH),
        ],
        out_specs=[piece(rows)] * 4
        + [summary] * 2
        + [tile(late, channels)]
        + [tile(late, states)] * 2
        + [whole(chunks, states, WIDTH)] * 2,
        out_shape=[wide_tokens] * 4
        + [like((spans, states, channels), F32)] * 2
        + [wide_tokens]
        + [like((tokens, states), F32)] * 2
        + [like((chunks, states, WIDTH), F32)] * 2,
        scratch_shapes=[
            pltpu.VMEM((rows + HALO, WIDTH), F32),
            scaled,
            scaled,
            pltpu.VMEM((8, WIDTH), F32),
            pltpu.VMEM((2, chunks, states, WIDTH), F32),
            pltpu.VMEM((2, chunks, 8, WIDTH), F32),
            slots,
            slots,
            pltpu.VMEM((HALO, channels), BF16),
            pltpu.SemaphoreType.DMA((2, chunks, rounds)),
            pltpu.SemaphoreType.DMA((2, chunks, rounds)),
            pltpu.SemaphoreType.DMA((2,)),
        ],
        compiler_params=pltpu.CompilerParams(
            vmem_limit_bytes=60 << 20,
            dimension_semantics=("arbitrary",),
            collective_id=0,
            has_side_effects=True,
        ),
        cost_estimate=cost(2 * span + 5 * states, 20 * size),
        name="fold",
    )(
        conv_input, conv_input, conv_input, grad_output, inject, readout, weights, wide,
        own_log.reshape(chunks, 1, WIDTH),
    )
    pairs, both = pl.pallas_call(
        shared_kernel,
        grid=(spans,),
        in_specs=[tile(back, channels)] * 4
        + [block(back, 1, channels)] * 2
        + [block(back, states, channels)] * 2
        + [whole(chunks, states, WIDTH)] * 2
        + [tile(back, states)] * 2,
        out_specs=[block(back, 2 * states, channels), tile(back, 2 * states)],
        out_shape=[
            like((spans, 2 * states, channels), BF16),
            like((tokens, 2 * states), F32),
        ],
        scratch_shapes=[
            pltpu.VMEM((2 * states, channels), BF16),
            pltpu.VMEM((states, channels), F32),
        ],
        compiler_params=params,
        cost_estimate=cost(8 * states, 14 * size),
        name="shared",
    )(grad_output, dg, act, da, lr, prior, before, fresh, entering, arriving, inner_b, inner_c)

    mine, pairs = lax.optimization_barrier((half_sums(both), pairs))
    grad_input, first = pl.pallas_call(
        input_kernel,
        grid=(spans,),
        in_specs=[
            tile(back, states),
            fixed(4),
            block(back, 1, channels),
            block(back, 2 * states, channels),
            tile(back, channels),
            tile(back, channels),
        ],
        out_specs=[tile(back, channels), fixed(8)],
        out_shape=[like((tokens, channels), F32), like((8, channels), F32)],
        scratch_shapes=[pltpu.VMEM((span + 8, channels), F32)],
        compiler_params=params,
        cost_estimate=cost(2 * states, 10 * size),
        name="inputs",
    )(inject, weights, lr, pairs, inner_act, slope)
    mine, first = lax.optimization_barrier((pair_sums(mine), first))
    later = shifted(first, "seq", -1)
    edge = jnp.stack(
        [sum(weights[k] * later[r - k] for k in range(r + 1)) for r in range(3)], axis=0
    )
    last = grad_input[tokens - 8 :] + jnp.pad(edge, ((5, 0), (0, 0)))
    grad_input = lax.dynamic_update_slice(grad_input, last, (tokens - 8, 0))
    total = joined_halves(mine)
    return grad_input, total[:, :states], total[:, states:]


def solution(mesh):
    return jax.shard_map(
        body,
        mesh=mesh,
        in_specs=(
            P("seq", "hg"),
            P("seq", "hg"),
            P("seq", None),
            P("seq", None),
            P(None, "hg"),
            P("hg", "seq"),
        ),
        out_specs=(P("seq", "hg"), P("seq", None), P("seq", None)),
        check_vma=False,
    )
```
